32 devices in a mesh: vid: 4 (over z), ty: 2 (over y), tx: 4 (over x, core).
Axes of the slice: x: 2, y: 2, z: 4, core: 2. Of those that a mesh axis runs over, the one named last changes fastest.
Arguments:
- latent_shards: bfloat16 [4, 99328], P('vid', ('ty', 'tx')), may hold values from -6 to 6
- shard_starts: int32 [4, 9], P('vid'), may hold values from 0 to 4096, as said below
- frame_dims: int32 [4, 2], P('vid'), may hold values from 16 to 128, as said below
- latent_cache: bfloat16 [4, 2, 32, 2048], P('vid', None, 'ty', 'tx'), may hold values from -6 to 6
- feature_cache: bfloat16 [4, 2, 32, 49152], P('vid', None, 'ty', 'tx'), may hold values from -5 to 5
- in_weight: bfloat16 [432, 384], replicated, may hold values from -0.3125 to 0.3125
- in_bias: float32 [384], replicated, may hold values from -3 to 3
- norm_gain: float32 [384], replicated, may hold values from 0.1 to 1.9
- res_weight: bfloat16 [10368, 384], replicated, may hold values from -0.0625 to 0.0625
- res_bias: float32 [384], replicated, may hold values from -3 to 3
- up_weight: bfloat16 [3456, 192], replicated, may hold values from -0.109375 to 0.109375
- up_bias: float32 [192], replicated, may hold values from -3 to 3
Outputs:
- decoded: bfloat16 [4, 64, 49152], P('vid', 'ty', 'tx')
The draws below stay inside these ranges and needn't reach their ends.
Inputs may be any that keep to these rules, and one draw needn't show every extreme that they name: `frame_dims`: row i gives video i's height, from 16 to 32, and width, from 64 to 128; one video fills the whole canvas and another is exactly 16 by 64. `shard_starts`: row i starts at 0, never falls, ends at video i's height times width, and every shard's token count fits its 776 slots; tokens lie in row-major order of the frame.
All inputs are finite; a program needn't handle non-finite values.
Results may differ from the reference program's by a relative error of at most 0.0095.
Values may be sent and summed in bfloat16 or wider, within the bound.
A program may use at most 64 MiB of HBM per device.

```python
import jax
import jax.numpy as jnp
from jax import lax

C = 384
Z = 16
CO = 192
VIDEOS = 4
SHARDS = 8
H_CAP = 32
W_CAP = 128
S_CAP = 776


def video_plan(key):
    base_key = jax.random.fold_in(key, 7)
    first_key, second_key, third_key, fourth_key = jax.random.split(base_key, 4)
    heights = jax.random.randint(first_key, (VIDEOS,), H_CAP // 2, H_CAP + 1)
    widths = jax.random.randint(second_key, (VIDEOS,), W_CAP // 2, W_CAP + 1)
    full_one = jax.random.randint(third_key, (), 0, VIDEOS)
    half_one = (full_one + 1) % VIDEOS
    labels = jnp.arange(VIDEOS, dtype=jnp.int32)
    heights = jnp.where(labels == full_one, H_CAP, jnp.where(labels == half_one, H_CAP // 2, heights)).astype(jnp.int32)
    widths = jnp.where(labels == full_one, W_CAP, jnp.where(labels == half_one, W_CAP // 2, widths)).astype(jnp.int32)
    totals = heights * widths
    base_count = totals // SHARDS
    jitter = jax.random.randint(fourth_key, (VIDEOS, SHARDS), 0, 1 << 20) % (base_count[:, None] // 2 + 1)
    counts = base_count[:, None] + jitter - jnp.roll(jitter, -1, axis=1)
    counts = counts.at[:, SHARDS - 1].add(totals - base_count * SHARDS)
    starts = jnp.concatenate([jnp.zeros((VIDEOS, 1), jnp.int32), jnp.cumsum(counts, axis=1).astype(jnp.int32)], axis=1)
    return (jnp.stack([heights, widths], axis=1).astype(jnp.int32), starts.astype(jnp.int32))


def draw_frame_dims(key, part):
    return video_plan(key)[0]


def draw_shard_starts(key, part):
    return video_plan(key)[1]


def block_levels(key, dims, pieces, smallest, high):
    loudness = 1.0
    for dim, shards_of in pieces:
        draws = jax.random.uniform(jax.random.fold_in(jax.random.fold_in(key, 6), dim), (shards_of,), jnp.float32, smallest / len(pieces), high / len(pieces))
        loudness = loudness * jnp.repeat(jnp.exp(draws), dims[dim] // shards_of).reshape((-1,) + (1,) * (len(dims) - 1 - dim))
    return loudness


def scatter_about(rng, dims, deviation, most, pieces=(), kind=jnp.bfloat16):
    values = deviation * jax.random.normal(rng, dims, jnp.float32)
    if pieces:
        values = values * block_levels(rng, dims, pieces, -0.22, 0.18)
    return jnp.clip(values, -most, most).astype(kind)


def setup_inputs(seed: int = 0) -> dict:
    arg_keys = jax.random.split(jax.random.key(seed), 13)
    latent_shards = scatter_about(arg_keys[0], (VIDEOS, SHARDS * S_CAP * Z), 1.0, 6.0, ((0, 4), (1, 8)))
    shard_starts = draw_shard_starts(jax.random.fold_in(arg_keys[12], 71), 0)
    frame_dims = draw_frame_dims(jax.random.fold_in(arg_keys[12], 71), 0)
    latent_cache = scatter_about(arg_keys[3], (VIDEOS, 2, H_CAP, W_CAP * Z), 1.0, 6.0, ((0, 4), (2, 2), (3, 4)))
    feature_cache = scatter_about(arg_keys[4], (VIDEOS, 2, H_CAP, W_CAP * C), 0.7, 5.0, ((0, 4), (2, 2), (3, 4)))
    in_weight = scatter_about(arg_keys[5], (27 * Z, C), (27 * Z) ** -0.5, 0.3125)
    in_bias = scatter_about(arg_keys[6], (C,), 0.5, 3.0, (), jnp.float32)
    norm_gain = jnp.clip(1.0 + 0.18 * jax.random.normal(arg_keys[7], (C,), jnp.float32), 0.1, 1.9)
    res_weight = scatter_about(arg_keys[8], (27 * C, C), (27 * C) ** -0.5, 0.0625)
    res_bias = scatter_about(arg_keys[9], (C,), 0.5, 3.0, (), jnp.float32)
    up_weight = scatter_about(arg_keys[10], (9 * C, CO), (9 * C) ** -0.5, 0.109375)
    up_bias = scatter_about(arg_keys[11], (CO,), 0.5, 3.0, (), jnp.float32)
    return {"latent_shards": latent_shards, "shard_starts": shard_starts, "frame_dims": frame_dims, "latent_cache": latent_cache, "feature_cache": feature_cache, "in_weight": in_weight, "in_bias": in_bias, "norm_gain": norm_gain, "res_weight": res_weight, "res_bias": res_bias, "up_weight": up_weight, "up_bias": up_bias}


EPS = 1e-06

def tap_sum(padded, weight, row_count, col_count):
    channels = padded.shape[-1]
    summed = jnp.zeros((row_count * col_count, weight.shape[1]), jnp.float32)
    for frame_at in range(padded.shape[0]):
        for row_at in range(3):
            for col_at in range(3):
                tap_index = (frame_at * 3 + row_at) * 3 + col_at
                window = padded[frame_at, row_at:row_at + row_count, col_at:col_at + col_count].reshape(row_count * col_count, channels)
                summed = summed + jnp.dot(window, weight[tap_index * channels:(tap_index + 1) * channels], preferred_element_type=jnp.float32)
    return summed

def conv_canvas(stacked, weight):
    padded = jnp.pad(stacked, ((0, 0), (1, 1), (1, 1), (0, 0)))
    return tap_sum(padded, weight, stacked.shape[1], stacked.shape[2])

def decode_video(shards, starts, frame, lat_old, feat_old, in_weight, in_bias, norm_gain, res_weight, res_bias, up_weight, up_bias):
    height = frame[0]
    breadth = frame[1]
    tokens = shards.reshape(SHARDS * S_CAP, Z)
    offset = jnp.arange(S_CAP, dtype=jnp.int32)
    counts = starts[1:] - starts[:-1]
    position = starts[:-1, None] + offset[None, :]
    live = offset[None, :] < counts[:, None]
    target = jnp.where(live, position // breadth * W_CAP + position % breadth, H_CAP * W_CAP).astype(jnp.int32)
    current = jnp.zeros((H_CAP * W_CAP, Z), jnp.bfloat16).at[target.reshape(-1)].set(tokens, mode='drop')
    ycoord = jnp.arange(H_CAP, dtype=jnp.int32)
    xcoord = jnp.arange(W_CAP, dtype=jnp.int32)
    keep = ((ycoord[:, None] < height) & (xcoord[None, :] < breadth)).astype(jnp.float32)
    keep_low = keep.astype(jnp.bfloat16)[None, :, :, None]
    keep_flat = keep.reshape(-1, 1)
    lat_stack = jnp.concatenate([lat_old.reshape(2, H_CAP, W_CAP, Z), current.reshape(1, H_CAP, W_CAP, Z)], 0) * keep_low
    first_out = (conv_canvas(lat_stack, in_weight) + in_bias).astype(jnp.bfloat16)
    values = first_out.astype(jnp.float32)
    power = lax.optimization_barrier(jnp.mean(values * values, axis=1, keepdims=True))
    normed = values * lax.rsqrt(power + EPS) * norm_gain
    hidden = (jax.nn.silu(normed) * keep_flat).astype(jnp.bfloat16)
    feat_stack = jnp.concatenate([feat_old.reshape(2, H_CAP, W_CAP, C) * keep_low, hidden.reshape(1, H_CAP, W_CAP, C)], 0)
    branch = conv_canvas(feat_stack, res_weight)
    mixed = ((values + branch + res_bias) * keep_flat).astype(jnp.bfloat16).reshape(H_CAP, W_CAP, C)
    grown = jnp.repeat(jnp.repeat(mixed, 2, axis=0), 2, axis=1)
    result = conv_canvas(grown[None], up_weight) + up_bias
    keep_high = jnp.repeat(jnp.repeat(keep, 2, axis=0), 2, axis=1).reshape(-1, 1)
    return (result * keep_high).astype(jnp.bfloat16).reshape(2 * H_CAP, 2 * W_CAP * CO)

def reference(latent_shards, shard_starts, frame_dims, latent_cache, feature_cache, in_weight, in_bias, norm_gain, res_weight, res_bias, up_weight, up_bias):

    def one_video(items):
        shards, starts, frame, lat_old, feat_old = items
        return decode_video(shards, starts, frame, lat_old, feat_old, in_weight, in_bias, norm_gain, res_weight, res_bias, up_weight, up_bias)
    return lax.map(one_video, (latent_shards, shard_starts, frame_dims, latent_cache, feature_cache))
```

```python
import functools

import jax
import jax.numpy as jnp
from jax import lax
from jax.experimental import pallas as pl
from jax.experimental.pallas import tpu as pltpu
from jax.sharding import PartitionSpec as P

EPS = 1e-06
F32 = jnp.float32
BF16 = jnp.bfloat16


def padded_2(value, sides, width):
    for axis, dim in sides:
        size, length = (lax.axis_size(axis), value.shape[dim])
        up = [(i, (i + 1) % size) for i in range(size - 1)]
        down = [(j, i) for i, j in up]
        wide = width[dim]
        last = lax.slice_in_dim(value, length - wide, length, axis=dim)
        leading = lax.slice_in_dim(value, 0, wide, axis=dim)
        before = lax.ppermute(last, axis, up)
        after = lax.ppermute(leading, axis, down)
        value = jnp.concatenate([before, value, after], axis=dim)
    return value


SLOT = 24
HIGH = 32


def compute_kernel(
    shards,
    starts_ref,
    dims_ref,
    tok_ref,
    lat_ref,
    feat_ref,
    in_w_ref,
    in_b_ref,
    gain_ref,
    res_w_ref,
    res_b_ref,
    up_w_ref,
    up_b_ref,
    out_ref,
    weights,
    toks,
    rows_s,
    lat_s,
    band,
    lat_lhs,
    upw,
    first_raw,
    stage,
    values,
    lhs,
    acc,
    grown,
    upacc,
    out_s,
    sems,
):
    channels = in_b_ref.shape[1]
    lanes = 3 * channels
    copies = []
    for f in range(3):
        for a in range(3):
            copy = pltpu.make_async_copy(
                res_w_ref.at[pl.ds((f * 3 + a) * lanes, lanes), :],
                weights.at[f, :, pl.ds(a * channels, channels)],
                sems.at[f * 3 + a],
            )
            copy.start()
            copies.append(copy)
    row0 = lax.axis_index("ty") * 16
    col0 = lax.axis_index("tx") * 32
    height = dims_ref[0, 0]
    breadth = dims_ref[0, 1]

    band[...] = jnp.zeros_like(band)
    for fa in range(9):
        block = in_w_ref[fa * 48 : fa * 48 + 48, :]
        for i in range(6):
            band[fa * 128 + i * 16 : fa * 128 + i * 16 + 48, i * channels : (i + 1) * channels] = (
                block
            )

    halves = (((0,), (1, 2)), ((0, 1), (2,)))

    def up_sum(pr, ar, pc, ac):
        total = None
        for a in halves[pr][ar]:
            for b in halves[pc][ac]:
                at = (a * 3 + b) * channels
                part = up_w_ref[at : at + channels, :].astype(F32)
                total = part if total is None else total + part
        return total

    for pr in range(2):
        for ar in range(2):
            near = jnp.concatenate([up_sum(pr, ar, 0, 1), up_sum(pr, ar, 1, 0)], axis=1)
            far = jnp.concatenate([up_sum(pr, ar, 0, 0), up_sum(pr, ar, 1, 1)], axis=1)
            upw[pr, ar * channels : (ar + 1) * channels, 0:channels] = near.astype(BF16)
            upw[pr, ar * channels : (ar + 1) * channels, channels : 2 * channels] = far.astype(
                BF16
            )

    token_rows = tok_ref.shape[1]
    for j in range(shards):
        toks[j] = jnp.zeros_like(toks[j])
        toks[j, 8 : 8 + token_rows, :] = tok_ref[j].astype(F32)
    lane = lax.broadcasted_iota(jnp.int32, (8, 128), 1)
    token = lax.broadcasted_iota(jnp.int32, (8, 128), 0) * 8 + lane // 16
    rows_s[...] = jnp.zeros_like(rows_s)

    def one_row(slab_row, carry):
        row = row0 + slab_row - 8
        first = row * breadth + col0 - 3
        col = token + (col0 - 3)
        place = token + first
        live = (col >= 0) & (col < breadth) & (row >= 0) & (row < height)
        picked = jnp.zeros((8, 128), F32)
        for j in range(shards):
            begin = starts_ref[0, j]
            end = starts_ref[0, j + 1]
            slot = jnp.clip(first - begin + 64, 0, (token_rows + 8) * 8)
            read = toks[j, pl.ds(slot >> 3, 8), :]
            shift = (slot & 7) * 16
            turned = pltpu.roll(read, lax.rem(128 - shift, 128), axis=1)
            after = pltpu.roll(turned, 7, axis=0)
            value = jnp.where(lane < 128 - shift, turned, after)
            picked = jnp.where((place >= begin) & (place < end), value, picked)
        rows_s[pl.ds(pl.multiple_of(slab_row * 8, 8), 8), :] = jnp.where(live, picked, 0.0)
        return carry

    lax.fori_loop(5, 27, one_row, 0)
    lat_lane = lax.broadcasted_iota(jnp.int32, (HIGH, 640), 1)
    lat_col = lat_lane // 16 + (col0 - 3)
    lat_row = lax.broadcasted_iota(jnp.int32, (HIGH, 640), 0) + (row0 - 8)
    lat_keep = (lat_row >= 0) & (lat_row < height) & (lat_col >= 0) & (lat_col < breadth)
    for f in range(2):
        lat_s[f] = jnp.where(lat_keep, lat_ref[f].astype(F32), 0.0)
    for g in range(5):
        lat_s[2, :, g * 128 : (g + 1) * 128] = rows_s[pl.ds(g, HIGH, stride=8), :]

    for f in range(3):
        frame = lat_s[f]
        for a in range(3):
            moved = frame if a == 1 else pltpu.roll(frame, 1 if a == 0 else HIGH - 1, axis=0)
            for g in range(6):
                lat_lhs[g * HIGH : (g + 1) * HIGH, (f * 3 + a) * 128 : (f * 3 + a + 1) * 128] = (
                    moved[:, g * 96 : g * 96 + 128].astype(BF16)
                )
    first_raw[...] = jnp.dot(lat_lhs[...], band[...], preferred_element_type=F32)

    slab_row = lax.broadcasted_iota(jnp.int32, (HIGH, channels), 0)
    row_ok = (slab_row + (row0 - 8) >= 0) & (slab_row + (row0 - 8) < height)
    row_ok_near = row_ok & (slab_row >= 6) & (slab_row < 26)
    eighth = lax.broadcasted_iota(jnp.int32, (8, channels), 0)

    def put_slab(dest, c, slab, before):
        head = slab[0:8] if before is None else jnp.where(eighth < 4, before, slab[0:8])
        dest[c * SLOT : c * SLOT + 8, :] = head
        dest[c * SLOT + 8 : c * SLOT + 24, :] = slab[8:24]
        return slab[24:32]

    def finish_lhs(f):
        for b in range(3):
            lhs[f, :, b * channels : (b + 1) * channels] = stage[
                b * SLOT : b * SLOT + lhs.shape[1], :
            ].astype(BF16)

    def col_ok(c):
        col = col0 - 2 + c
        return (col >= 0) & (col < breadth)

    tail = jnp.zeros((8, channels), F32)
    stage[36 * SLOT + 8 :, :] = jnp.zeros((stage.shape[0] - 36 * SLOT - 8, channels), F32)
    for f in range(2):
        before = tail
        for c in range(36):
            slab = feat_ref[f, :, c * channels : (c + 1) * channels].astype(F32)
            slab = jnp.where(row_ok_near & col_ok(c), slab, 0.0)
            before = put_slab(stage, c, slab, before)
        stage[36 * SLOT : 36 * SLOT + 8, :] = before
        finish_lhs(f)
    in_b = in_b_ref[...]
    gain = gain_ref[...]
    before = tail
    before_values = tail
    for c in range(36):
        g, i = c // 6, c % 6
        raw = first_raw[g * HIGH : (g + 1) * HIGH, i * channels : (i + 1) * channels]
        value = (raw + in_b).astype(BF16).astype(F32)
        power = jnp.mean(value * value, axis=1, keepdims=True)
        normed = value * lax.rsqrt(power + EPS) * gain
        hidden = normed / (1.0 + jnp.exp(-normed))
        hidden = jnp.where(row_ok_near & col_ok(c), hidden, 0.0)
        before = put_slab(stage, c, hidden, before)
        before_values = put_slab(values, c, value, before_values)
    stage[36 * SLOT : 36 * SLOT + 8, :] = before
    values[36 * SLOT : 36 * SLOT + 8, :] = before_values
    finish_lhs(2)

    for copy in copies:
        copy.wait()

    def frame_dot(f, carry):
        part = jnp.dot(lhs[f], weights[f], preferred_element_type=F32)

        @pl.when(f == 0)
        def _():
            acc[...] = part

        @pl.when(f > 0)
        def _():
            acc[...] += part

        return carry

    lax.fori_loop(0, 3, frame_dot, 0)

    res_b = res_b_ref[...]
    for c in range(34):
        rows = pl.ds(c * SLOT, HIGH)
        slab = acc[rows, channels : 2 * channels]
        slab += pltpu.roll(acc[rows, 0:channels], 1, axis=0)
        slab += pltpu.roll(acc[rows, 2 * channels :], HIGH - 1, axis=0)
        slab += values[pl.ds((c + 1) * SLOT, HIGH), :]
        slab = jnp.where(row_ok & col_ok(c + 1), slab + res_b, 0.0)
        at = c * 16
        grown[at : at + 16, 0:channels] = pltpu.roll(slab, 1, axis=0)[8:24].astype(BF16)
        grown[at : at + 16, channels : 2 * channels] = slab[8:24].astype(BF16)
        grown[at : at + 16, 2 * channels :] = pltpu.roll(slab, HIGH - 1, axis=0)[8:24].astype(BF16)

    up_b = jnp.concatenate([up_b_ref[...], up_b_ref[...]], axis=1)
    left = lax.broadcasted_iota(jnp.int32, (16, channels), 1) < channels // 2
    own_row = row_ok[8:24]
    for pr in range(2):
        upacc[...] = jnp.dot(
            grown[:, pr * channels : (pr + 2) * channels], upw[pr], preferred_element_type=F32
        )
        for j in range(32):
            centre = upacc[(j + 1) * 16 : (j + 2) * 16, 0:channels]
            west = upacc[j * 16 : (j + 1) * 16, channels:]
            east = upacc[(j + 2) * 16 : (j + 3) * 16, channels:]
            slab = centre + jnp.where(left, west, east) + up_b
            slab = jnp.where(own_row & col_ok(j + 2), slab, 0.0)
            for k in range(channels // 128):
                out_s[j * 3 + k, pl.ds(pr, 16, stride=2), :] = slab[:, k * 128 : (k + 1) * 128]
    for j in range(32 * 3):
        out_ref[:, j * 128 : (j + 1) * 128] = out_s[j].astype(BF16)


def compute(shards, starts, dims, tok, lat, feat, weights):
    in_w, in_b, gain, res_w, res_b, up_w, up_b = weights
    channels = in_b.shape[0]
    out_width = up_b.shape[0]
    cells = 34 * SLOT + 16
    vmem = pl.BlockSpec(memory_space=pltpu.VMEM)
    smem = pl.BlockSpec(memory_space=pltpu.SMEM)
    return pl.pallas_call(
        functools.partial(compute_kernel, shards),
        out_shape=jax.ShapeDtypeStruct((32, 64 * out_width), BF16),
        in_specs=[smem, smem, vmem, vmem, vmem, vmem, vmem, vmem]
        + [pl.BlockSpec(memory_space=pl.ANY), vmem, vmem, vmem],
        out_specs=vmem,
        scratch_shapes=[
            pltpu.VMEM((3, 3 * channels, 3 * channels), BF16),
            pltpu.VMEM((shards, (tok.shape[1] + 16 + 15) // 8 * 8, 128), F32),
            pltpu.VMEM((HIGH * 8, 128), F32),
            pltpu.VMEM((3, HIGH, 640), F32),
            pltpu.VMEM((9 * 128, 6 * channels), BF16),
            pltpu.VMEM((6 * HIGH, 9 * 128), BF16),
            pltpu.VMEM((2, 2 * channels, 2 * channels), BF16),
            pltpu.VMEM((6 * HIGH, 6 * channels), F32),
            pltpu.VMEM((cells + 2 * SLOT, channels), F32),
            pltpu.VMEM((cells + 2 * SLOT, channels), F32),
            pltpu.VMEM((3, cells, 3 * channels), BF16),
            pltpu.VMEM((cells, 3 * channels), F32),
            pltpu.VMEM((34 * 16, 3 * channels), BF16),
            pltpu.VMEM((34 * 16, 2 * channels), F32),
            pltpu.VMEM((32 * 3, 32, 128), F32),
            pltpu.SemaphoreType.DMA((9,)),
        ],
        compiler_params=pltpu.CompilerParams(vmem_limit_bytes=56 * 1024 * 1024),
        cost_estimate=pl.CostEstimate(
            flops=9_000_000_000, bytes_accessed=13_000_000, transcendentals=400_000
        ),
    )(
        starts,
        dims,
        tok,
        lat,
        feat,
        in_w,
        in_b.reshape(1, -1),
        gain.reshape(1, -1),
        res_w,
        res_b.reshape(1, -1),
        up_w,
        up_b.reshape(1, -1),
    )


def per_device(
    latent_shards,
    shard_starts,
    frame_dims,
    latent_cache,
    feature_cache,
    *weights,
):
    channels = weights[1].shape[0]
    latent_width = weights[0].shape[0] // 27
    shard_count = lax.axis_size("ty") * lax.axis_size("tx")
    tok = lax.all_gather(latent_shards, ("ty", "tx"), axis=1, tiled=True)
    tok = tok.reshape(shard_count, -1, 128)
    sides = (("ty", 1), ("tx", 2))
    lat = padded_2(latent_cache[0], sides, {1: 3, 2: 3 * latent_width})
    lat = jnp.pad(lat, ((0, 0), (5, 5), (0, 32)))
    feat = padded_2(feature_cache[0], sides, {1: 2, 2: 2 * channels})
    feat = jnp.pad(feat, ((0, 0), (6, 6), (0, 0)))
    out = compute(shard_count, shard_starts, frame_dims, tok, lat, feat, weights)
    return out[None]


def solution(mesh):
    return jax.shard_map(
        per_device,
        mesh=mesh,
        in_specs=(
            P("vid", ("ty", "tx")),
            P("vid", None),
            P("vid", None),
            P("vid", None, "ty", "tx"),
            P("vid", None, "ty", "tx"),
            P(),
            P(),
            P(),
            P(),
            P(),
            P(),
            P(),
        ),
        out_specs=P("vid", "ty", "tx"),
        check_vma=False,
    )
```

```python
import functools

import jax
import jax.numpy as jnp
from jax import lax
from jax.experimental import pallas as pl
from jax.experimental.pallas import tpu as pltpu
from jax.sharding import PartitionSpec as P

EPS = 1e-06
F32 = jnp.float32
BF16 = jnp.bfloat16


NEAR = ((-1, -1), (-1, 0), (-1, 1), (0, -1), (0, 1), (1, -1), (1, 0), (1, 1))


SLOT = 24
HIGH = 32


def compute_kernel(
    down_count,
    across,
    starts_ref,
    dims_ref,
    own_tok_ref,
    lat_ref,
    feat_ref,
    in_w_ref,
    in_b_ref,
    gain_ref,
    res_w_ref,
    res_b_ref,
    up_w_ref,
    up_b_ref,
    out_ref,
    weights,
    tok_pack,
    tok_all,
    lat_rows,
    lat_sides,
    feat_rows,
    feat_sides,
    feat_corners,
    row_pack,
    toks,
    rows_s,
    lat_s,
    band,
    lat_lhs,
    upw,
    first_raw,
    stage,
    values,
    lhs,
    acc,
    grown,
    upacc,
    out_s,
    sems,
    tok_send,
    tok_recv,
    feat_send,
    feat_recv,
    lat_send,
    lat_recv,
):
    channels = in_b_ref.shape[0]
    lanes = 3 * channels
    shards = down_count * across
    ty = lax.axis_index("ty")
    tx = lax.axis_index("tx")
    myself = ty * across + tx
    mesh_ids = pl.DeviceIdType.MESH

    def peer(step):
        other = lax.rem(myself + step, shards)
        return {"ty": other // across, "tx": lax.rem(other, across)}

    barrier = pltpu.get_barrier_semaphore()
    for step in range(1, shards):
        pl.semaphore_signal(barrier, inc=1, device_id=peer(step), device_id_type=mesh_ids)

    copies = []
    for f in range(3):
        for a in range(3):
            copy = pltpu.make_async_copy(
                res_w_ref.at[pl.ds((f * 3 + a) * lanes, lanes), :],
                weights.at[f, :, pl.ds(a * channels, channels)],
                sems.at[f * 3 + a],
            )
            copy.start()
            copies.append(copy)

    token_rows = own_tok_ref.shape[1] // 128
    tok_pack[...] = jnp.zeros_like(tok_pack)
    for k in range(token_rows):
        tok_pack[k : k + 1, :] = own_tok_ref[:, k * 128 : (k + 1) * 128].astype(F32)
    tok_all[myself] = tok_pack[...].astype(BF16)

    quarter = feat_ref.shape[2] // 4
    pack_row = lax.broadcasted_iota(jnp.int32, (16, quarter), 0) // 2
    for side in range(2):
        packed = jnp.zeros((16, quarter), F32)
        for k in range(4):
            for f in range(2):
                piece = feat_ref[f, :, k * quarter : (k + 1) * quarter].astype(F32)
                turn = (4 * k + 2 * f - 14 * side) % 16
                if turn:
                    piece = pltpu.roll(piece, turn, axis=0)
                packed = jnp.where(pack_row == 2 * k + f, piece, packed)
        row_pack[side] = packed.astype(BF16)

    pl.semaphore_wait(barrier, shards - 1)

    def token_copy(step):
        return pltpu.make_async_remote_copy(
            src_ref=tok_all.at[myself],
            dst_ref=tok_all.at[myself],
            send_sem=tok_send.at[step],
            recv_sem=tok_recv.at[step],
            device_id=peer(step),
            device_id_type=mesh_ids,
        )

    def token_arrival(step):
        source = lax.rem(myself + shards - step, shards)
        return pltpu.make_async_remote_copy(
            src_ref=tok_all.at[source],
            dst_ref=tok_all.at[source],
            send_sem=tok_send.at[step],
            recv_sem=tok_recv.at[step],
            device_id=peer(step),
            device_id_type=mesh_ids,
        )

    def near_copies(at, land, target):
        dy, dx = NEAR[at]
        side = (dy + 1) // 2
        edge = 2 * channels
        lat_piece = lat_ref.at[:, :, pl.ds(0 if dx < 0 else lat_ref.shape[2] - 128, 128)]
        if dy == 0:
            first = 0 if dx < 0 else feat_ref.shape[2] - edge
            feat_pair = (feat_ref.at[:, :, pl.ds(first, edge)], feat_sides.at[land - 3])
        elif dx == 0:
            feat_pair = (row_pack.at[side], feat_rows.at[0 if land == 1 else 1])
        else:
            first = 0 if dx < 0 else quarter - edge
            feat_pair = (row_pack.at[side, :, pl.ds(first, edge)], feat_corners.at[land])
        if dx == 0:
            lat_pair = (lat_ref, lat_rows.at[0 if land == 1 else 1])
        else:
            lat_pair = (lat_piece, lat_sides.at[land])
        made = []
        for (src, dst), send, recv in (
            (feat_pair, feat_send, feat_recv),
            (lat_pair, lat_send, lat_recv),
        ):
            made.append(
                pltpu.make_async_remote_copy(
                    src_ref=src,
                    dst_ref=dst,
                    send_sem=send.at[at],
                    recv_sem=recv.at[land],
                    device_id={"ty": ty + NEAR[target][0], "tx": tx + NEAR[target][1]},
                    device_id_type=mesh_ids,
                )
            )
        return made

    def if_near(at, act):
        dy, dx = NEAR[at]
        there = (ty + dy >= 0) & (ty + dy < down_count) & (tx + dx >= 0) & (tx + dx < across)
        pl.when(there)(act)

    for step in range(1, shards):
        token_copy(step).start()
    for at in range(8):

        def send_near(at=at):
            for copy in near_copies(at, 7 - at, at):
                copy.start()

        if_near(at, send_near)

    row0 = ty * 16
    col0 = tx * 32
    height = dims_ref[0, 0]
    breadth = dims_ref[0, 1]

    band[...] = jnp.zeros_like(band)
    for fa in range(9):
        block = in_w_ref[fa * 48 : fa * 48 + 48, :]
        for i in range(6):
            band[fa * 128 + i * 16 : fa * 128 + i * 16 + 48, i * channels : (i + 1) * channels] = (
                block
            )

    halves = (((0,), (1, 2)), ((0, 1), (2,)))
    out_width = up_w_ref.shape[0]
    for pr in range(2):
        for ar in range(2):
            for part, (pc, ac) in enumerate(((0, 1), (1, 0), (0, 0), (1, 1))):
                total = None
                for a in halves[pr][ar]:
                    for b in halves[pc][ac]:
                        at = (a * 3 + b) * channels
                        tap = up_w_ref[:, at : at + channels].astype(F32)
                        total = tap if total is None else total + tap
                upw[
                    pr,
                    part * out_width : (part + 1) * out_width,
                    ar * channels : (ar + 1) * channels,
                ] = total.astype(BF16)

    for step in range(1, shards):
        token_copy(step).wait_send()
        token_arrival(step).wait_recv()
    for at in range(8):

        def wait_near(at=at):
            for copy in near_copies(at, 7 - at, at):
                copy.wait_send()
            for copy in near_copies(7 - at, at, at):
                copy.wait_recv()

        if_near(at, wait_near)

    for j in range(shards):
        toks[j, 0:8, :] = jnp.zeros((8, 128), F32)
        toks[j, 8 : 8 + tok_all.shape[1], :] = tok_all[j].astype(F32)
    lane = lax.broadcasted_iota(jnp.int32, (8, 128), 1)
    token = lax.broadcasted_iota(jnp.int32, (8, 128), 0) * 8 + lane // 16
    rows_s[...] = jnp.zeros_like(rows_s)

    def one_row(slab_row, carry):
        row = row0 + slab_row - 8
        first = row * breadth + col0 - 3
        col = token + (col0 - 3)
        place = token + first
        live = (col >= 0) & (col < breadth) & (row >= 0) & (row < height)
        picked = jnp.zeros((8, 128), F32)
        for j in range(shards):
            begin = starts_ref[0, j]
            end = starts_ref[0, j + 1]
            slot = jnp.clip(first - begin + 64, 0, (token_rows + 8) * 8)
            read = toks[j, pl.ds(slot >> 3, 8), :]
            shift = (slot & 7) * 16
            turned = pltpu.roll(read, lax.rem(128 - shift, 128), axis=1)
            after = pltpu.roll(turned, 7, axis=0)
            value = jnp.where(lane < 128 - shift, turned, after)
            picked = jnp.where((place >= begin) & (place < end), value, picked)
        rows_s[pl.ds(pl.multiple_of(slab_row * 8, 8), 8), :] = jnp.where(live, picked, 0.0)
        return carry

    lax.fori_loop(5, 27, one_row, 0)
    lat_lane = lax.broadcasted_iota(jnp.int32, (HIGH, 640), 1)
    lat_col = lat_lane // 16 + (col0 - 3)
    lat_row = lax.broadcasted_iota(jnp.int32, (HIGH, 640), 0) + (row0 - 8)
    lat_keep = (lat_row >= 0) & (lat_row < height) & (lat_col >= 0) & (lat_col < breadth)
    for f in range(2):
        blocks = []
        for west, centre, east in (
            (lat_sides[0, f], lat_rows[0, f], lat_sides[2, f]),
            (lat_sides[3, f], lat_ref[f], lat_sides[4, f]),
            (lat_sides[5, f], lat_rows[1, f], lat_sides[7, f]),
        ):
            wide = jnp.concatenate(
                [west.astype(F32), centre.astype(F32), east.astype(F32)], axis=1
            )
            blocks.append(pltpu.roll(wide, 768 - 80, axis=1)[:, :640])
        tall = jnp.concatenate([blocks[0][8:16], blocks[1], blocks[2][0:8]], axis=0)
        lat_s[f] = jnp.where(lat_keep, tall, 0.0)
    for g in range(5):
        lat_s[2, :, g * 128 : (g + 1) * 128] = rows_s[pl.ds(g, HIGH, stride=8), :]

    for f in range(3):
        frame = lat_s[f]
        for a in range(3):
            moved = frame if a == 1 else pltpu.roll(frame, 1 if a == 0 else HIGH - 1, axis=0)
            for g in range(6):
                lat_lhs[g * HIGH : (g + 1) * HIGH, (f * 3 + a) * 128 : (f * 3 + a + 1) * 128] = (
                    moved[:, g * 96 : g * 96 + 128].astype(BF16)
                )
    first_raw[...] = jnp.dot(lat_lhs[...], band[...], preferred_element_type=F32)

    slab_row = lax.broadcasted_iota(jnp.int32, (HIGH, channels), 0)
    row_ok = (slab_row + (row0 - 8) >= 0) & (slab_row + (row0 - 8) < height)
    row_ok_near = row_ok & (slab_row >= 6) & (slab_row < 26)
    eighth = lax.broadcasted_iota(jnp.int32, (8, channels), 0)

    def put_slab(dest, c, slab, before):
        head = slab[0:8] if before is None else jnp.where(eighth < 4, before, slab[0:8])
        dest[c * SLOT : c * SLOT + 8, :] = head
        dest[c * SLOT + 8 : c * SLOT + 24, :] = slab[8:24]
        return slab[24:32]

    def finish_lhs(f):
        for b in range(3):
            lhs[f, :, b * channels : (b + 1) * channels] = stage[
                b * SLOT : b * SLOT + lhs.shape[1], :
            ].astype(BF16)

    def col_ok(c):
        col = col0 - 2 + c
        return (col >= 0) & (col < breadth)

    def packed_rows(rows_at, corner_at, f, c, land):
        if c < 2:
            col, lane0, held = 30 + c, c, feat_corners.at[corner_at]
        elif c < 34:
            col, lane0, held = c - 2, (c - 2) % 8, feat_rows.at[rows_at]
        else:
            col, lane0, held = c - 34, c - 34, feat_corners.at[corner_at + 2]
        piece = held[:, lane0 * channels : (lane0 + 1) * channels].astype(F32)
        turn = (land - (col // 8) * 4 - f * 2) % 16
        if turn:
            piece = pltpu.roll(piece, turn, axis=0)
        return piece[0:8]

    def feature_slab(f, c):
        if c < 2:
            middle = feat_sides[0, f, :, c * channels : (c + 1) * channels]
        elif c < 34:
            middle = feat_ref[f, :, (c - 2) * channels : (c - 1) * channels]
        else:
            middle = feat_sides[1, f, :, (c - 34) * channels : (c - 33) * channels]
        above = packed_rows(0, 0, f, c, 6)
        below = packed_rows(1, 5, f, c, 0)
        return jnp.concatenate([above, middle.astype(F32), below], axis=0)

    tail = jnp.zeros((8, channels), F32)
    stage[36 * SLOT + 8 :, :] = jnp.zeros((stage.shape[0] - 36 * SLOT - 8, channels), F32)
    for f in range(2):
        before = tail
        for c in range(36):
            slab = feature_slab(f, c)
            slab = jnp.where(row_ok_near & col_ok(c), slab, 0.0)
            before = put_slab(stage, c, slab, before)
        stage[36 * SLOT : 36 * SLOT + 8, :] = before
        finish_lhs(f)
    in_b = in_b_ref[...].reshape(1, channels)
    gain = gain_ref[...].reshape(1, channels)
    before = tail
    before_values = tail
    for c in range(36):
        g, i = c // 6, c % 6
        raw = first_raw[g * HIGH : (g + 1) * HIGH, i * channels : (i + 1) * channels]
        value = (raw + in_b).astype(BF16).astype(F32)
        power = jnp.mean(value * value, axis=1, keepdims=True)
        normed = value * lax.rsqrt(power + EPS) * gain
        hidden = normed / (1.0 + jnp.exp(-normed))
        hidden = jnp.where(row_ok_near & col_ok(c), hidden, 0.0)
        before = put_slab(stage, c, hidden, before)
        before_values = put_slab(values, c, value, before_values)
    stage[36 * SLOT : 36 * SLOT + 8, :] = before
    values[36 * SLOT : 36 * SLOT + 8, :] = before_values
    finish_lhs(2)

    for copy in copies:
        copy.wait()

    def frame_dot(f, carry):
        part = jnp.dot(lhs[f], weights[f], preferred_element_type=F32)

        @pl.when(f == 0)
        def _():
            acc[...] = part

        @pl.when(f > 0)
        def _():
            acc[...] += part

        return carry

    lax.fori_loop(0, 3, frame_dot, 0)

    res_b = res_b_ref[...].reshape(1, channels)
    for c in range(34):
        rows = pl.ds(c * SLOT, HIGH)
        slab = acc[rows, channels : 2 * channels]
        slab += pltpu.roll(acc[rows, 0:channels], 1, axis=0)
        slab += pltpu.roll(acc[rows, 2 * channels :], HIGH - 1, axis=0)
        slab += values[pl.ds((c + 1) * SLOT, HIGH), :]
        slab = jnp.where(row_ok & col_ok(c + 1), slab + res_b, 0.0)
        at = c * 16
        grown[at : at + 16, 0:channels] = pltpu.roll(slab, 1, axis=0)[8:24].astype(BF16)
        grown[at : at + 16, channels : 2 * channels] = slab[8:24].astype(BF16)
        grown[at : at + 16, 2 * channels :] = pltpu.roll(slab, HIGH - 1, axis=0)[8:24].astype(BF16)

    up_b = jnp.concatenate([up_b_ref[...].reshape(1, out_width)] * 2, axis=1)
    left = lax.broadcasted_iota(jnp.int32, (16, channels), 1) < channels // 2
    own_row = row_ok[8:24]
    for pr in range(2):
        upacc[...] = lax.dot_general(
            grown[:, pr * channels : (pr + 2) * channels],
            upw[pr],
            (((1,), (1,)), ((), ())),
            preferred_element_type=F32,
        )
        for j in range(32):
            centre = upacc[(j + 1) * 16 : (j + 2) * 16, 0:channels]
            west = upacc[j * 16 : (j + 1) * 16, channels:]
            east = upacc[(j + 2) * 16 : (j + 3) * 16, channels:]
            slab = centre + jnp.where(left, west, east) + up_b
            slab = jnp.where(own_row & col_ok(j + 2), slab, 0.0)
            for k in range(channels // 128):
                out_s[j * 3 + k, pl.ds(pr, 16, stride=2), :] = slab[:, k * 128 : (k + 1) * 128]
    for j in range(32 * 3):
        out_ref[0, :, j * 128 : (j + 1) * 128] = out_s[j].astype(BF16)


def per_device(
    latent_shards,
    shard_starts,
    frame_dims,
    latent_cache,
    feature_cache,
    in_weight,
    in_bias,
    norm_gain,
    res_weight,
    res_bias,
    up_weight,
    up_bias,
):
    channels = in_bias.shape[0]
    out_width = up_bias.shape[0]
    down_count = lax.axis_size("ty")
    across = lax.axis_size("tx")
    shards = down_count * across
    token_rows = (latent_shards.shape[1] // 128 + 15) // 16 * 16
    cells = 34 * SLOT + 16
    vmem = pl.BlockSpec(memory_space=pltpu.VMEM)
    smem = pl.BlockSpec(memory_space=pltpu.SMEM)
    return pl.pallas_call(
        functools.partial(compute_kernel, down_count, across),
        out_shape=jax.ShapeDtypeStruct((1, 32, 64 * out_width), BF16),
        in_specs=[smem, smem, vmem, vmem, vmem, vmem, vmem, vmem]
        + [pl.BlockSpec(memory_space=pl.ANY), vmem, vmem, vmem],
        out_specs=vmem,
        scratch_shapes=[
            pltpu.VMEM((3, 3 * channels, 3 * channels), BF16),
            pltpu.VMEM((token_rows, 128), F32),
            pltpu.VMEM((shards, token_rows, 128), BF16),
            pltpu.VMEM((2, 2, 16, 512), BF16),
            pltpu.VMEM((8, 2, 16, 128), BF16),
            pltpu.VMEM((2, 16, 8 * channels), BF16),
            pltpu.VMEM((2, 2, 16, 2 * channels), BF16),
            pltpu.VMEM((8, 16, 2 * channels), BF16),
            pltpu.VMEM((2, 16, 8 * channels), BF16),
            pltpu.VMEM((shards, token_rows + 16, 128), F32),
            pltpu.VMEM((HIGH * 8, 128), F32),
            pltpu.VMEM((3, HIGH, 640), F32),
            pltpu.VMEM((9 * 128, 6 * channels), BF16),
            pltpu.VMEM((6 * HIGH, 9 * 128), BF16),
            pltpu.VMEM((2, 4 * out_width, 2 * channels), BF16),
            pltpu.VMEM((6 * HIGH, 6 * channels), F32),
            pltpu.VMEM((cells + 2 * SLOT, channels), F32),
            pltpu.VMEM((cells + 2 * SLOT, channels), F32),
            pltpu.VMEM((3, cells, 3 * channels), BF16),
            pltpu.VMEM((cells, 3 * channels), F32),
            pltpu.VMEM((34 * 16, 3 * channels), BF16),
            pltpu.VMEM((34 * 16, 2 * channels), F32),
            pltpu.VMEM((32 * 3, 32, 128), F32),
            pltpu.SemaphoreType.DMA((9,)),
            pltpu.SemaphoreType.DMA((shards,)),
            pltpu.SemaphoreType.DMA((shards,)),
            pltpu.SemaphoreType.DMA((8,)),
            pltpu.SemaphoreType.DMA((8,)),
            pltpu.SemaphoreType.DMA((8,)),
            pltpu.SemaphoreType.DMA((8,)),
        ],
        compiler_params=pltpu.CompilerParams(
            vmem_limit_bytes=56 * 1024 * 1024, collective_id=0, has_side_effects=True
        ),
        cost_estimate=pl.CostEstimate(
            flops=9_000_000_000, bytes_accessed=13_000_000, transcendentals=400_000
        ),
    )(
        shard_starts,
        frame_dims,
        latent_shards,
        latent_cache[0],
        feature_cache[0],
        in_weight,
        in_bias,
        norm_gain,
        res_weight,
        res_bias,
        up_weight.T,
        up_bias,
    )


def solution(mesh):
    return jax.shard_map(
        per_device,
        mesh=mesh,
        in_specs=(
            P("vid", ("ty", "tx")),
            P("vid", None),
            P("vid", None),
            P("vid", None, "ty", "tx"),
            P("vid", None, "ty", "tx"),
            P(),
            P(),
            P(),
            P(),
            P(),
            P(),
            P(),
        ),
        out_specs=P("vid", "ty", "tx"),
        check_vma=False,
    )
```

```python
import functools

import jax
import jax.numpy as jnp
from jax import lax
from jax.experimental import pallas as pl
from jax.experimental.pallas import tpu as pltpu
from jax.sharding import PartitionSpec as P

EPS = 1e-06
F32 = jnp.float32
BF16 = jnp.bfloat16


NEAR = ((-1, -1), (-1, 0), (-1, 1), (0, -1), (0, 1), (1, -1), (1, 0), (1, 1))


SLOT = 24
HIGH = 32


def compute_kernel(
    down_count,
    across,
    starts_ref,
    dims_ref,
    own_tok_ref,
    lat_ref,
    feat_ref,
    in_w_ref,
    in_b_ref,
    gain_ref,
    res_w_ref,
    res_b_ref,
    up_w_ref,
    up_b_ref,
    out_ref,
    weights,
    tok_pack,
    tok_all,
    lat_rows,
    lat_sides,
    feat_rows,
    feat_sides,
    feat_corners,
    row_pack,
    toks,
    rows_s,
    lat_s,
    band,
    lat_lhs,
    upw,
    first_raw,
    stage,
    values,
    lhs,
    acc,
    grown,
    upacc,
    out_s,
    sems,
    tok_send,
    tok_recv,
    feat_send,
    feat_recv,
    lat_send,
    lat_recv,
):
    channels = in_b_ref.shape[0]
    lanes = 3 * channels
    shards = down_count * across
    ty = lax.axis_index("ty")
    tx = lax.axis_index("tx")
    myself = ty * across + tx
    mesh_ids = pl.DeviceIdType.MESH

    def peer(step):
        other = lax.rem(myself + step, shards)
        return {"ty": other // across, "tx": lax.rem(other, across)}

    barrier = pltpu.get_barrier_semaphore()
    for step in range(1, shards):
        pl.semaphore_signal(barrier, inc=1, device_id=peer(step), device_id_type=mesh_ids)

    copies = []
    for f in range(3):
        for a in range(3):
            copy = pltpu.make_async_copy(
                res_w_ref.at[pl.ds((f * 3 + a) * lanes, lanes), :],
                weights.at[f, :, pl.ds(a * channels, channels)],
                sems.at[f * 3 + a],
            )
            copy.start()
            copies.append(copy)

    token_rows = own_tok_ref.shape[1] // 128
    tok_pack[...] = jnp.zeros_like(tok_pack)
    for k in range(token_rows):
        tok_pack[k : k + 1, :] = own_tok_ref[:, k * 128 : (k + 1) * 128].astype(F32)
    tok_all[myself] = tok_pack[...].astype(BF16)

    quarter = feat_ref.shape[2] // 4
    pl.semaphore_wait(barrier, shards - 1)

    def token_copy(step):
        return pltpu.make_async_remote_copy(
            src_ref=tok_all.at[myself],
            dst_ref=tok_all.at[myself],
            send_sem=tok_send.at[step],
            recv_sem=tok_recv.at[step],
            device_id=peer(step),
            device_id_type=mesh_ids,
        )

    def token_arrival(step):
        source = lax.rem(myself + shards - step, shards)
        return pltpu.make_async_remote_copy(
            src_ref=tok_all.at[source],
            dst_ref=tok_all.at[source],
            send_sem=tok_send.at[step],
            recv_sem=tok_recv.at[step],
            device_id=peer(step),
            device_id_type=mesh_ids,
        )

    def near_copies(at, land, target):
        dy, dx = NEAR[at]
        side = (dy + 1) // 2
        edge = 2 * channels
        lat_piece = lat_ref.at[:, :, pl.ds(0 if dx < 0 else lat_ref.shape[2] - 128, 128)]
        if dy == 0:
            first = 0 if dx < 0 else feat_ref.shape[2] - edge
            feat_pair = (feat_ref.at[:, :, pl.ds(first, edge)], feat_sides.at[land - 3])
        elif dx == 0:
            feat_pair = (row_pack.at[side], feat_rows.at[0 if land == 1 else 1])
        else:
            first = 0 if dx < 0 else quarter - edge
            feat_pair = (row_pack.at[side, :, pl.ds(first, edge)], feat_corners.at[land])
        if dx == 0:
            lat_pair = (lat_ref, lat_rows.at[0 if land == 1 else 1])
        else:
            lat_pair = (lat_piece, lat_sides.at[land])
        made = []
        for (src, dst), send, recv in (
            (feat_pair, feat_send, feat_recv),
            (lat_pair, lat_send, lat_recv),
        ):
            made.append(
                pltpu.make_async_remote_copy(
                    src_ref=src,
                    dst_ref=dst,
                    send_sem=send.at[at],
                    recv_sem=recv.at[land],
                    device_id={"ty": ty + NEAR[target][0], "tx": tx + NEAR[target][1]},
                    device_id_type=mesh_ids,
                )
            )
        return made

    def if_near(at, act):
        dy, dx = NEAR[at]
        there = (ty + dy >= 0) & (ty + dy < down_count) & (tx + dx >= 0) & (tx + dx < across)
        pl.when(there)(act)

    for step in range(1, shards):
        token_copy(step).start()
    def send_near(kind):
        for at in range(8):

            def send_one(at=at):
                near_copies(at, 7 - at, at)[kind].start()

            if_near(at, send_one)

    send_near(1)
    pack_row = lax.broadcasted_iota(jnp.int32, (16, quarter), 0) // 2
    for side in range(2):
        packed = jnp.zeros((16, quarter), F32)
        for k in range(4):
            for f in range(2):
                piece = feat_ref[f, :, k * quarter : (k + 1) * quarter].astype(F32)
                turn = (4 * k + 2 * f - 14 * side) % 16
                if turn:
                    piece = pltpu.roll(piece, turn, axis=0)
                packed = jnp.where(pack_row == 2 * k + f, piece, packed)
        row_pack[side] = packed.astype(BF16)
    send_near(0)

    row0 = ty * 16
    col0 = tx * 32
    height = dims_ref[0, 0]
    breadth = dims_ref[0, 1]

    band[...] = jnp.zeros_like(band)
    for fa in range(9):
        block = in_w_ref[fa * 48 : fa * 48 + 48, :]
        for i in range(6):
            band[fa * 128 + i * 16 : fa * 128 + i * 16 + 48, i * channels : (i + 1) * channels] = (
                block
            )

    halves = (((0,), (1, 2)), ((0, 1), (2,)))
    out_width = up_w_ref.shape[0]
    for pr in range(2):
        for ar in range(2):
            for part, (pc, ac) in enumerate(((0, 1), (1, 0), (0, 0), (1, 1))):
                total = None
                for a in halves[pr][ar]:
                    for b in halves[pc][ac]:
                        at = (a * 3 + b) * channels
                        tap = up_w_ref[:, at : at + channels].astype(F32)
                        total = tap if total is None else total + tap
                upw[
                    pr,
                    part * out_width : (part + 1) * out_width,
                    ar * channels : (ar + 1) * channels,
                ] = total.astype(BF16)

    for step in range(1, shards):
        token_copy(step).wait_send()
        token_arrival(step).wait_recv()
    def wait_near(kind):
        for at in range(8):

            def wait_one(at=at):
                near_copies(at, 7 - at, at)[kind].wait_send()
                near_copies(7 - at, at, at)[kind].wait_recv()

            if_near(at, wait_one)


    for j in range(shards):
        toks[j, 0:8, :] = jnp.zeros((8, 128), F32)
        toks[j, 8 : 8 + tok_all.shape[1], :] = tok_all[j].astype(F32)
    lane = lax.broadcasted_iota(jnp.int32, (8, 128), 1)
    token = lax.broadcasted_iota(jnp.int32, (8, 128), 0) * 8 + lane // 16
    rows_s[...] = jnp.zeros_like(rows_s)

    def one_row(slab_row, carry):
        row = row0 + slab_row - 8
        first = row * breadth + col0 - 3
        col = token + (col0 - 3)
        place = token + first
        live = (col >= 0) & (col < breadth) & (row >= 0) & (row < height)
        picked = jnp.zeros((8, 128), F32)
        for j in range(shards):
            begin = starts_ref[0, j]
            end = starts_ref[0, j + 1]
            slot = jnp.clip(first - begin + 64, 0, (token_rows + 8) * 8)
            read = toks[j, pl.ds(slot >> 3, 8), :]
            shift = (slot & 7) * 16
            turned = pltpu.roll(read, lax.rem(128 - shift, 128), axis=1)
            after = pltpu.roll(turned, 7, axis=0)
            value = jnp.where(lane < 128 - shift, turned, after)
            picked = jnp.where((place >= begin) & (place < end), value, picked)
        rows_s[pl.ds(pl.multiple_of(slab_row * 8, 8), 8), :] = jnp.where(live, picked, 0.0)
        return carry

    lax.fori_loop(5, 27, one_row, 0)
    wait_near(1)
    lat_lane = lax.broadcasted_iota(jnp.int32, (HIGH, 640), 1)
    lat_col = lat_lane // 16 + (col0 - 3)
    lat_row = lax.broadcasted_iota(jnp.int32, (HIGH, 640), 0) + (row0 - 8)
    lat_keep = (lat_row >= 0) & (lat_row < height) & (lat_col >= 0) & (lat_col < breadth)
    for f in range(2):
        blocks = []
        for west, centre, east in (
            (lat_sides[0, f], lat_rows[0, f], lat_sides[2, f]),
            (lat_sides[3, f], lat_ref[f], lat_sides[4, f]),
            (lat_sides[5, f], lat_rows[1, f], lat_sides[7, f]),
        ):
            wide = jnp.concatenate(
                [west.astype(F32), centre.astype(F32), east.astype(F32)], axis=1
            )
            blocks.append(pltpu.roll(wide, 768 - 80, axis=1)[:, :640])
        tall = jnp.concatenate([blocks[0][8:16], blocks[1], blocks[2][0:8]], axis=0)
        lat_s[f] = jnp.where(lat_keep, tall, 0.0)
    for g in range(5):
        lat_s[2, :, g * 128 : (g + 1) * 128] = rows_s[pl.ds(g, HIGH, stride=8), :]

    for f in range(3):
        frame = lat_s[f]
        for a in range(3):
            moved = frame if a == 1 else pltpu.roll(frame, 1 if a == 0 else HIGH - 1, axis=0)
            for g in range(6):
                lat_lhs[g * HIGH : (g + 1) * HIGH, (f * 3 + a) * 128 : (f * 3 + a + 1) * 128] = (
                    moved[:, g * 96 : g * 96 + 128].astype(BF16)
                )
    first_raw[...] = jnp.dot(lat_lhs[...], band[...], preferred_element_type=F32)

    slab_row = lax.broadcasted_iota(jnp.int32, (HIGH, channels), 0)
    row_ok = (slab_row + (row0 - 8) >= 0) & (slab_row + (row0 - 8) < height)
    row_ok_near = row_ok & (slab_row >= 6) & (slab_row < 26)
    eighth = lax.broadcasted_iota(jnp.int32, (8, channels), 0)

    def put_slab(dest, c, slab, before):
        head = slab[0:8] if before is None else jnp.where(eighth < 4, before, slab[0:8])
        dest[c * SLOT : c * SLOT + 8, :] = head
        dest[c * SLOT + 8 : c * SLOT + 24, :] = slab[8:24]
        return slab[24:32]

    def finish_lhs(f):
        for b in range(3):
            lhs[f, :, b * channels : (b + 1) * channels] = stage[
                b * SLOT : b * SLOT + lhs.shape[1], :
            ].astype(BF16)

    def col_ok(c):
        col = col0 - 2 + c
        return (col >= 0) & (col < breadth)

    def packed_rows(rows_at, corner_at, f, c, land):
        if c < 2:
            col, lane0, held = 30 + c, c, feat_corners.at[corner_at]
        elif c < 34:
            col, lane0, held = c - 2, (c - 2) % 8, feat_rows.at[rows_at]
        else:
            col, lane0, held = c - 34, c - 34, feat_corners.at[corner_at + 2]
        piece = held[:, lane0 * channels : (lane0 + 1) * channels].astype(F32)
        turn = (land - (col // 8) * 4 - f * 2) % 16
        if turn:
            piece = pltpu.roll(piece, turn, axis=0)
        return piece[0:8]

    def feature_slab(f, c):
        if c < 2:
            middle = feat_sides[0, f, :, c * channels : (c + 1) * channels]
        elif c < 34:
            middle = feat_ref[f, :, (c - 2) * channels : (c - 1) * channels]
        else:
            middle = feat_sides[1, f, :, (c - 34) * channels : (c - 33) * channels]
        above = packed_rows(0, 0, f, c, 6)
        below = packed_rows(1, 5, f, c, 0)
        return jnp.concatenate([above, middle.astype(F32), below], axis=0)

    tail = jnp.zeros((8, channels), F32)
    stage[36 * SLOT + 8 :, :] = jnp.zeros((stage.shape[0] - 36 * SLOT - 8, channels), F32)
    in_b = in_b_ref[...].reshape(1, channels)
    gain = gain_ref[...].reshape(1, channels)
    before = tail
    before_values = tail
    for c in range(36):
        g, i = c // 6, c % 6
        raw = first_raw[g * HIGH : (g + 1) * HIGH, i * channels : (i + 1) * channels]
        value = (raw + in_b).astype(BF16).astype(F32)
        power = jnp.mean(value * value, axis=1, keepdims=True)
        normed = value * lax.rsqrt(power + EPS) * gain
        hidden = normed / (1.0 + jnp.exp(-normed))
        hidden = jnp.where(row_ok_near & col_ok(c), hidden, 0.0)
        before = put_slab(stage, c, hidden, before)
        before_values = put_slab(values, c, value, before_values)
    stage[36 * SLOT : 36 * SLOT + 8, :] = before
    values[36 * SLOT : 36 * SLOT + 8, :] = before_values
    finish_lhs(2)

    for copy in copies:
        copy.wait()
    acc[...] = jnp.dot(lhs[2], weights[2], preferred_element_type=F32)
    wait_near(0)
    for f in range(2):
        before = tail
        for c in range(36):
            slab = feature_slab(f, c)
            slab = jnp.where(row_ok_near & col_ok(c), slab, 0.0)
            before = put_slab(stage, c, slab, before)
        stage[36 * SLOT : 36 * SLOT + 8, :] = before
        finish_lhs(f)

    def frame_dot(f, carry):
        acc[...] += jnp.dot(lhs[f], weights[f], preferred_element_type=F32)
        return carry

    lax.fori_loop(0, 2, frame_dot, 0)

    res_b = res_b_ref[...].reshape(1, channels)
    for c in range(34):
        rows = pl.ds(c * SLOT, HIGH)
        slab = acc[rows, channels : 2 * channels]
        slab += pltpu.roll(acc[rows, 0:channels], 1, axis=0)
        slab += pltpu.roll(acc[rows, 2 * channels :], HIGH - 1, axis=0)
        slab += values[pl.ds((c + 1) * SLOT, HIGH), :]
        slab = jnp.where(row_ok & col_ok(c + 1), slab + res_b, 0.0)
        at = c * 16
        grown[at : at + 16, 0:channels] = pltpu.roll(slab, 1, axis=0)[8:24].astype(BF16)
        grown[at : at + 16, channels : 2 * channels] = slab[8:24].astype(BF16)
        grown[at : at + 16, 2 * channels :] = pltpu.roll(slab, HIGH - 1, axis=0)[8:24].astype(BF16)

    up_b = jnp.concatenate([up_b_ref[...].reshape(1, out_width)] * 2, axis=1)
    left = lax.broadcasted_iota(jnp.int32, (16, channels), 1) < channels // 2
    own_row = row_ok[8:24]
    for pr in range(2):
        upacc[...] = lax.dot_general(
            grown[:, pr * channels : (pr + 2) * channels],
            upw[pr],
            (((1,), (1,)), ((), ())),
            preferred_element_type=F32,
        )
        for j in range(32):
            centre = upacc[(j + 1) * 16 : (j + 2) * 16, 0:channels]
            west = upacc[j * 16 : (j + 1) * 16, channels:]
            east = upacc[(j + 2) * 16 : (j + 3) * 16, channels:]
            slab = centre + jnp.where(left, west, east) + up_b
            slab = jnp.where(own_row & col_ok(j + 2), slab, 0.0)
            for k in range(channels // 128):
                out_s[j * 3 + k, pl.ds(pr, 16, stride=2), :] = slab[:, k * 128 : (k + 1) * 128]
    for j in range(32 * 3):
        out_ref[0, :, j * 128 : (j + 1) * 128] = out_s[j].astype(BF16)


def per_device(
    latent_shards,
    shard_starts,
    frame_dims,
    latent_cache,
    feature_cache,
    in_weight,
    in_bias,
    norm_gain,
    res_weight,
    res_bias,
    up_weight,
    up_bias,
):
    channels = in_bias.shape[0]
    out_width = up_bias.shape[0]
    down_count = lax.axis_size("ty")
    across = lax.axis_size("tx")
    shards = down_count * across
    token_rows = (latent_shards.shape[1] // 128 + 15) // 16 * 16
    cells = 34 * SLOT + 16
    vmem = pl.BlockSpec(memory_space=pltpu.VMEM)
    smem = pl.BlockSpec(memory_space=pltpu.SMEM)
    return pl.pallas_call(
        functools.partial(compute_kernel, down_count, across),
        out_shape=jax.ShapeDtypeStruct((1, 32, 64 * out_width), BF16),
        in_specs=[smem, smem, vmem, vmem, vmem, vmem, vmem, vmem]
        + [pl.BlockSpec(memory_space=pl.ANY), vmem, vmem, vmem],
        out_specs=vmem,
        scratch_shapes=[
            pltpu.VMEM((3, 3 * channels, 3 * channels), BF16),
            pltpu.VMEM((token_rows, 128), F32),
            pltpu.VMEM((shards, token_rows, 128), BF16),
            pltpu.VMEM((2, 2, 16, 512), BF16),
            pltpu.VMEM((8, 2, 16, 128), BF16),
            pltpu.VMEM((2, 16, 8 * channels), BF16),
            pltpu.VMEM((2, 2, 16, 2 * channels), BF16),
            pltpu.VMEM((8, 16, 2 * channels), BF16),
            pltpu.VMEM((2, 16, 8 * channels), BF16),
            pltpu.VMEM((shards, token_rows + 16, 128), F32),
            pltpu.VMEM((HIGH * 8, 128), F32),
            pltpu.VMEM((3, HIGH, 640), F32),
            pltpu.VMEM((9 * 128, 6 * channels), BF16),
            pltpu.VMEM((6 * HIGH, 9 * 128), BF16),
            pltpu.VMEM((2, 4 * out_width, 2 * channels), BF16),
            pltpu.VMEM((6 * HIGH, 6 * channels), F32),
            pltpu.VMEM((cells + 2 * SLOT, channels), F32),
            pltpu.VMEM((cells + 2 * SLOT, channels), F32),
            pltpu.VMEM((3, cells, 3 * channels), BF16),
            pltpu.VMEM((cells, 3 * channels), F32),
            pltpu.VMEM((34 * 16, 3 * channels), BF16),
            pltpu.VMEM((34 * 16, 2 * channels), F32),
            pltpu.VMEM((32 * 3, 32, 128), F32),
            pltpu.SemaphoreType.DMA((9,)),
            pltpu.SemaphoreType.DMA((shards,)),
            pltpu.SemaphoreType.DMA((shards,)),
            pltpu.SemaphoreType.DMA((8,)),
            pltpu.SemaphoreType.DMA((8,)),
            pltpu.SemaphoreType.DMA((8,)),
            pltpu.SemaphoreType.DMA((8,)),
        ],
        compiler_params=pltpu.CompilerParams(
            vmem_limit_bytes=56 * 1024 * 1024, collective_id=0, has_side_effects=True
        ),
        cost_estimate=pl.CostEstimate(
            flops=9_000_000_000, bytes_accessed=13_000_000, transcendentals=400_000
        ),
    )(
        shard_starts,
        frame_dims,
        latent_shards,
        latent_cache[0],
        feature_cache[0],
        in_weight,
        in_bias,
        norm_gain,
        res_weight,
        res_bias,
        up_weight.T,
        up_bias,
    )


def solution(mesh):
    return jax.shard_map(
        per_device,
        mesh=mesh,
        in_specs=(
            P("vid", ("ty", "tx")),
            P("vid", None),
            P("vid", None),
            P("vid", None, "ty", "tx"),
            P("vid", None, "ty", "tx"),
            P(),
            P(),
            P(),
            P(),
            P(),
            P(),
            P(),
        ),
        out_specs=P("vid", "ty", "tx"),
        check_vma=False,
    )
```
